32 devices in a mesh: groups: 2 (over x), blk: 8 (over z, y), rows: 2 (over core).
Axes of the slice: x: 2, y: 2, z: 4, core: 2. Of those that a mesh axis runs over, the one named last changes fastest.
Arguments:
- queries: bfloat16 [256, 2048], P(('groups', 'blk'), 'rows'), parts along dimension 0, may hold values from -170 to 170
- cache_keys: bfloat16 [8192, 256], P(('groups', 'blk'), 'rows'), parts along dimension 0, may hold values from -6 to 6
- cache_values: bfloat16 [8192, 256], P(('groups', 'blk'), 'rows'), parts along dimension 0, may hold values from -6 to 6
- span_starts: int32 [4], P('groups'), parts along dimension 0, may hold values from 0 to 4032, as said below
- out_weight: bfloat16 [2048, 2048], P(('rows', 'blk')), may hold values from -0.125 to 0.125
- norm_gain: bfloat16 [2048], replicated, may hold values from 0.099609375 to 1.8984375
- expert_ids: int32 [256, 8], P(('groups', 'blk', 'rows')), parts along dimension 0, may hold values from 0 to 15, all different within a row; in each aligned block of 8 rows (0 to 7, 8 to 15, ...) at most 8 rows name the same one
- gate_fixed: int32 [256, 8], P(('groups', 'blk', 'rows')), parts along dimension 0, may hold values from 1 to 4095
- gate_weight: bfloat16 [16, 2048, 768], P(('blk', 'rows')), may hold values from -0.125 to 0.125
- up_weight: bfloat16 [16, 2048, 768], P(('blk', 'rows')), may hold values from -0.125 to 0.125
- down_weight: bfloat16 [16, 768, 2048], P(('blk', 'rows')), may hold values from -0.21875 to 0.21875
Outputs:
- attn_proj: bfloat16 [256, 2048], P(('groups', 'blk', 'rows')), parts along dimension 0
- expert_out: bfloat16 [256, 2048], P(('groups', 'blk', 'rows')), parts along dimension 0
The draws below stay inside these ranges and needn't reach their ends.
There are 2 independent parts, one for each index of `groups`. The reference program is written for one: setup_inputs(seed, part) draws one part's arguments, and reference() takes and returns one part's arrays. A program takes and returns all parts, laid end to end along the dimension named above; an argument that names none is the same for every part. Nothing has to cross between parts.
Inputs may be any that keep to these rules, and one draw needn't show every extreme that they name: `span_starts`: the last span ends at the last cached position, entry 1 is 4032; entry 0 is at most 3968. `expert_ids`: each token names 8 different experts; among the tokens of one device (aligned blocks of 8 rows) no expert is named more than 8 times.
All inputs are finite; a program needn't handle non-finite values.
Results may differ from the reference program's by a relative error of at most 0.035.
Values may be sent and summed in bfloat16 or wider, within the bound.
A program may use at most 64 MiB of HBM per device.

```python
import math
import jax
import jax.numpy as jnp
import numpy as np
from jax import lax

D = 2048
QH = 16
KVH = 2
HD = 128
FF_E = 768
TOP = 8
CACHE_DEV = 512
QTOK = 128
SPAN_LEN = 64
CACHE = 4096
MOE_TOK = 8
EXPERTS = 16
CAP = 8
N_BLK = 8


def spike_plan(key):
    base_keys = jax.random.normal(jax.random.fold_in(key, 101), (CACHE, KVH * HD), jnp.float32)
    base_keys = jnp.clip(base_keys, -6.0, 6.0)
    return base_keys


def draw_cache_keys(key, part):
    base_keys = spike_plan(key)
    return base_keys.astype(jnp.bfloat16)


def draw_queries(key, part):
    fresh = jax.random.normal(jax.random.fold_in(key, 103), (QTOK, QH * HD), jnp.float32)
    fresh = jnp.clip(fresh, -6.0, 6.0) * 3.0
    return fresh.astype(jnp.bfloat16)


def draw_span_starts(key, part):
    first = jax.random.randint(jax.random.fold_in(key, 105), (1,), 0, CACHE - 2 * SPAN_LEN + 1)
    last = jnp.full((1,), CACHE - SPAN_LEN, jnp.int32)
    return jnp.concatenate([first.astype(jnp.int32), last]).astype(jnp.int32)


def set_ends(result, key, low, high):
    spot = [jax.random.randint(jax.random.fold_in(key, axis), (), 0, length) for axis, length in enumerate(result.shape)]
    main_axis = result.shape.index(max(result.shape))
    beside = spot[:main_axis] + [(spot[main_axis] + 1) % result.shape[main_axis]] + spot[main_axis + 1:]
    return result.at[tuple(spot)].set(low).at[tuple(beside)].set(high)


def block_levels(own_key, dims, cuts, least, largest):
    def one(axis_at, blocks):
        steps = jax.random.uniform(jax.random.fold_in(jax.random.fold_in(own_key, 6), axis_at), (blocks,), jnp.float32, least / len(cuts), largest / len(cuts))
        return jnp.repeat(jnp.exp(steps), dims[axis_at] // blocks).reshape((-1,) + (1,) * (len(dims) - axis_at - 1))

    factor_of = one(*cuts[0])
    for cut in cuts[1:]:
        factor_of = factor_of * one(*cut)
    return factor_of


def routed_block(own_key, own, number, rows, amount, top, limit, slope):
    ranking = jax.random.permutation(own_key, amount)
    crowded, ordinary = portions_of(amount, rows * top, limit, slope, True), portions_of(amount, rows * top, limit, slope, False)
    places = jnp.arange(amount)

    def named(sizes, turn):
        used = int((sizes > 0).sum())
        fixed = max(1, used // 4)
        passed = fixed + (places - fixed + turn * (used - fixed)) % max(1, amount - fixed)
        return jnp.zeros((amount,), jnp.int32).at[ranking[jnp.where(places < fixed, places, passed)]].set(jnp.asarray(sizes, jnp.int32))

    sizes = jnp.where(number % 4 == 0, named(crowded, number // 4), named(ordinary, number - number // 4 - 1))
    mixed = jax.random.permutation(jax.random.fold_in(own, 3), amount)
    giver, taker = mixed[0:amount // 2 * 2:2], mixed[1:amount // 2 * 2:2]
    slack = jnp.minimum(sizes[giver] - 1, limit - sizes[taker]) // 2
    slack = jnp.where((giver == ranking[0]) | (taker == ranking[0]) | (sizes[taker] == 0), 0, jnp.maximum(slack, 0))
    passed = jax.random.randint(jax.random.fold_in(own, 4), (amount // 2,), 0, 1 << 20) % (slack + 1)
    sizes = sizes.at[giver].add(-passed).at[taker].add(passed)
    members = jnp.searchsorted(jnp.cumsum(sizes), jnp.arange(rows * top), side="right").astype(jnp.int32)
    table = members.reshape(top, rows).T
    table = table[jax.random.permutation(jax.random.fold_in(own, 1), rows)]
    turn = jax.random.randint(jax.random.fold_in(own, 2), (rows, 1), 0, top)
    return jnp.take_along_axis(table, (jnp.arange(top)[None, :] + turn) % top, axis=1)


def portions_of(count, total, most, slope, full):
    portions = [(1 << 20) // math.isqrt(grade ** slope) + 1 for grade in range(1, count + 1)]
    largest = most if full else min(most, max(-(-total // count), total * portions[0] // sum(portions)))
    least = 1 if total - largest >= count - 1 else 0
    holding, spare = [largest] + [least] * (count - 1), total - largest - least * (count - 1)
    while spare > 0:
        movable = [i for i in range(1, count) if holding[i] < largest] or [i for i in range(1, count) if holding[i] < most]
        whole, left = sum([portions[i] for i in movable]), spare
        for i in movable:
            more = min(most - holding[i], max(1, left * portions[i] // whole), spare)
            holding[i] = holding[i] + more
            spare = spare - more
    return np.array(holding)


def centred(rng, extent, scale, bound, split=(), held_as=jnp.bfloat16):
    level = block_levels(rng, extent, split, -0.22, 0.18) if split else 1.0
    values = jax.random.normal(rng, extent, jnp.float32) * scale * level
    return jnp.minimum(jnp.maximum(values, -bound), bound).astype(held_as)


def setup_inputs(seed: int = 0, part: int = 0) -> dict:
    seeds = jax.random.split(jax.random.key(seed), 12)
    part_splits = jax.random.split(jax.random.fold_in(seeds[11], part), 12)
    queries = draw_queries(jax.random.fold_in(jax.random.fold_in(seeds[11], part), 71), part)
    cache_keys = draw_cache_keys(jax.random.fold_in(jax.random.fold_in(seeds[11], part), 71), part)
    cache_values = centred(part_splits[2], (CACHE, KVH * HD), 1.0, 6.0, ((0, 8), (1, 2)))
    span_starts = draw_span_starts(jax.random.fold_in(jax.random.fold_in(seeds[11], part), 71), part)
    out_weight = centred(seeds[4], (QH * HD, D), (QH * HD) ** -0.5, 0.125, ((0, 16),))
    norm_gain = jnp.clip(1.0 + 0.18 * jax.random.normal(seeds[5], (D,), jnp.float32), 0.099609375, 1.8984375).astype(jnp.bfloat16)
    expert_ids_keys = jax.random.split(jax.random.fold_in(part_splits[6], 1), QTOK // MOE_TOK)
    expert_ids_turns = jax.random.permutation(jax.random.fold_in(part_splits[6], 3), QTOK // MOE_TOK)
    expert_ids = jax.vmap(lambda own, number: routed_block(jax.random.fold_in(part_splits[6], 2), own, number, MOE_TOK, EXPERTS, TOP, CAP, 0))(expert_ids_keys, expert_ids_turns).reshape((QTOK, TOP))
    gate_fixed = set_ends(jax.random.randint(part_splits[7], (QTOK, TOP), 1, 4096), jax.random.fold_in(part_splits[7], 1), 1, 4095).astype(jnp.int32)
    gate_weight = centred(seeds[8], (EXPERTS, D, FF_E), D ** -0.5, 0.125, ((0, 16),))
    up_weight = centred(seeds[9], (EXPERTS, D, FF_E), D ** -0.5, 0.125, ((0, 16),))
    down_weight = centred(seeds[10], (EXPERTS, FF_E, D), FF_E ** -0.5, 0.21875, ((0, 16),))
    return {"queries": queries, "cache_keys": cache_keys, "cache_values": cache_values, "span_starts": span_starts, "out_weight": out_weight, "norm_gain": norm_gain, "expert_ids": expert_ids, "gate_fixed": gate_fixed, "gate_weight": gate_weight, "up_weight": up_weight, "down_weight": down_weight}


NEG_FILL = -1e+30
EPSILON = 1e-06

def reference(queries, cache_keys, cache_values, span_starts, out_weight, norm_gain, expert_ids, gate_fixed, gate_weight, up_weight, down_weight):
    group_size = QH // KVH
    token_index = jnp.arange(QTOK, dtype=jnp.int32)
    query_pos = span_starts[token_index // SPAN_LEN] + token_index % SPAN_LEN
    query_f = queries.astype(jnp.float32).reshape(QTOK, KVH, group_size, HD)
    key_blocks = cache_keys.reshape(N_BLK, CACHE_DEV, KVH, HD)
    value_blocks = cache_values.reshape(N_BLK, CACHE_DEV, KVH, HD)
    score_scale = 1.0 / math.sqrt(HD)

    def one_block(running, item):
        best, numerator, totals = running
        key_block, value_block, block_number = item
        key_pos = block_number * CACHE_DEV + jnp.arange(CACHE_DEV, dtype=jnp.int32)
        visible = (key_pos[None, :] <= query_pos[:, None])[:, None, None, :]
        scores = jnp.einsum('qgjd,kgd->qgjk', query_f, key_block.astype(jnp.float32)) * score_scale
        scores = jnp.where(visible, scores, NEG_FILL)
        block_top = lax.optimization_barrier(jnp.max(scores, axis=-1))
        weights = jnp.where(visible, jnp.exp(scores - block_top[..., None]), 0.0)
        block_sum = lax.optimization_barrier(jnp.sum(weights, axis=-1))
        rounded = weights.astype(jnp.bfloat16).astype(jnp.float32)
        block_out = jnp.einsum('qgjk,kgd->qgjd', rounded, value_block.astype(jnp.float32))
        newest = jnp.maximum(best, block_top)
        old_factor = jnp.exp(best - newest)
        new_factor = jnp.exp(block_top - newest)
        numerator = numerator * old_factor[..., None] + block_out * new_factor[..., None]
        totals = totals * old_factor + block_sum * new_factor
        return ((newest, numerator, totals), None)
    start_best = jnp.full((QTOK, KVH, group_size), NEG_FILL, jnp.float32)
    start_numer = jnp.zeros((QTOK, KVH, group_size, HD), jnp.float32)
    start_totals = jnp.zeros((QTOK, KVH, group_size), jnp.float32)
    block_ids = jnp.arange(N_BLK, dtype=jnp.int32)
    final, unused = lax.scan(one_block, (start_best, start_numer, start_totals), (key_blocks, value_blocks, block_ids))
    attention = (final[1] / final[2][..., None]).reshape(QTOK, QH * HD).astype(jnp.bfloat16)
    attn_proj = jnp.dot(attention, out_weight, preferred_element_type=jnp.float32).astype(jnp.bfloat16)
    values_f = attn_proj.astype(jnp.float32)
    mean_square = lax.optimization_barrier(jnp.mean(values_f * values_f, axis=-1, keepdims=True))
    normed = (values_f * lax.rsqrt(mean_square + EPSILON) * norm_gain.astype(jnp.float32)).astype(jnp.bfloat16)
    gate_values = gate_fixed.astype(jnp.float32)
    route_weight = gate_values / lax.optimization_barrier(jnp.sum(gate_values, axis=1, keepdims=True))

    def one_expert(total, item):
        expert_gate, expert_up, expert_down, expert_number = item
        gate_part = jnp.dot(normed, expert_gate, preferred_element_type=jnp.float32)
        up_part = jnp.dot(normed, expert_up, preferred_element_type=jnp.float32)
        expert_hidden = (jax.nn.silu(gate_part) * up_part).astype(jnp.bfloat16)
        expert_result = jnp.dot(expert_hidden, expert_down, preferred_element_type=jnp.float32).astype(jnp.bfloat16)
        weight_sum = lax.optimization_barrier(jnp.sum(jnp.where(expert_ids == expert_number, route_weight, 0.0), axis=1))
        return (total + weight_sum[:, None] * expert_result.astype(jnp.float32), None)
    expert_numbers = jnp.arange(EXPERTS, dtype=jnp.int32)
    start_total = jnp.zeros((QTOK, D), jnp.float32)
    mixed, unused_two = lax.scan(one_expert, start_total, (gate_weight, up_weight, down_weight, expert_numbers))
    expert_out = mixed.astype(jnp.bfloat16)
    return (attn_proj, expert_out)
```

```python
import functools
import math

import jax
import jax.numpy as jnp
from jax import lax
from jax.experimental import pallas as pl
from jax.experimental.pallas import tpu as pltpu
from jax.sharding import PartitionSpec as P

HD = 128
NEG_FILL = -1e30
EPSILON = 1e-06
LANES = 128
PARTS = 2
MESH = pl.DeviceIdType.MESH
F32 = jnp.float32
BF16 = jnp.bfloat16


def fused(
    n,
    q_hbm,
    k_hbm,
    v_hbm,
    starts,
    ow_hbm,
    gain_ref,
    ids_ref,
    gates_ref,
    g_hbm,
    u_hbm,
    d_hbm,
    proj_ref,
    out_ref,
    qbuf,
    kbuf,
    vbuf,
    owbuf,
    gbuf,
    ubuf,
    dbuf,
    wbuf,
    num_send,
    num_recv,
    st_send,
    st_recv,
    att_rows,
    sib_send,
    sib_recv,
    acc,
    red_send,
    red_recv,
    xbuf,
    xs,
    local_sem,
    q_sems,
    w_sems,
    num_sems,
    st_sems,
    red_sems,
    x_sems,
    fwd_sems,
    sib_sems,
    wf_sems,
):
    b = lax.axis_index("blk")
    r = lax.axis_index("rows")
    other = 1 - r
    own_q, width = q_hbm.shape
    rows_t = n * own_q
    tokens = own_q // 2
    heads = width // HD
    cw = width // n
    per_head = HD // cw
    keys = k_hbm.shape[0]
    d_model = ow_hbm.shape[1]
    half = d_model // 2
    part = half // PARTS
    spans = starts.shape[0]

    def peer(j):
        return lax.rem(b + j, n)

    loads = [
        pltpu.make_async_copy(src, dst, local_sem.at[i])
        for i, (src, dst) in enumerate(
            (
                (q_hbm, qbuf.at[b]),
                (k_hbm, kbuf),
                (v_hbm, vbuf),
                (ow_hbm, owbuf),
                (g_hbm.at[0], gbuf),
                (u_hbm.at[0], ubuf),
                (d_hbm.at[0], dbuf),
            )
        )
    ]
    for load in loads:
        load.start()

    barrier = pltpu.get_barrier_semaphore()

    def greet(j, carry):
        pl.semaphore_signal(barrier, inc=1, device_id={"blk": peer(j)}, device_id_type=MESH)
        return carry

    lax.fori_loop(1, n, greet, 0)
    pl.semaphore_signal(barrier, inc=1, device_id={"rows": other}, device_id_type=MESH)

    gates = gates_ref[...].astype(F32)
    share = gates / jnp.sum(gates, axis=1, keepdims=True)
    ids = ids_ref[...]
    lane = lax.broadcasted_iota(jnp.int32, wbuf.shape[2:], 1)
    table = jnp.zeros(wbuf.shape[2:], F32)
    for k in range(ids_ref.shape[1]):
        table = table + jnp.where(ids[:, k : k + 1] == lane, share[:, k : k + 1], 0.0)
    wbuf[r, b] = table

    pl.semaphore_wait(barrier, n)

    def to_peer(src, dst, sems, p, slot):
        return pltpu.make_async_remote_copy(
            src_ref=src,
            dst_ref=dst,
            send_sem=sems.at[0, p],
            recv_sem=sems.at[1, slot],
            device_id={"blk": p},
            device_id_type=MESH,
        )

    def to_sibling(src, dst, send_sem, recv_sem):
        return pltpu.make_async_remote_copy(
            src_ref=src,
            dst_ref=dst,
            send_sem=send_sem,
            recv_sem=recv_sem,
            device_id={"rows": other},
            device_id_type=MESH,
        )

    def q_copy(p, slot):
        return to_peer(q_hbm, qbuf.at[slot], q_sems, p, slot)

    def w_copy(p, slot):
        return to_peer(wbuf.at[r, slot], wbuf.at[r, slot], w_sems, p, slot)

    def send_queries(j, carry):
        q_copy(peer(j), b).start()
        return carry

    def send_table(j, carry):
        w_copy(peer(j), b).start()
        return carry

    lax.fori_loop(1, n, send_queries, 0)
    lax.fori_loop(1, n, send_table, 0)

    loads[0].wait()
    loads[1].wait()
    loads[2].wait()
    key_block = kbuf[...]
    value_t = vbuf[...].T

    token = lax.broadcasted_iota(jnp.int32, (1, rows_t), 1)
    span_len = rows_t // spans
    start_of = jnp.zeros((1, rows_t), jnp.int32)
    for s in range(spans):
        start_of = jnp.where(token // span_len == s, starts[s], start_of)
    query_pos = start_of + lax.rem(token, span_len)
    limit = query_pos - b * keys
    visible = lax.broadcasted_iota(jnp.int32, (keys, rows_t), 0) <= limit

    def wait_queries(j, carry):
        q_copy(b, peer(j)).wait_recv()
        return carry

    lax.fori_loop(1, n, wait_queries, 0)

    def num_copy(p, slot):
        return to_peer(num_send.at[p], num_recv.at[slot], num_sems, p, slot)

    def st_copy(h, p, slot):
        return to_peer(st_send.at[h], st_recv.at[slot], st_sems, p, slot)

    scale = 1.0 / math.sqrt(HD)
    for j in range(heads):
        h = lax.rem(b // per_head + 1 + j, heads)
        q_h = qbuf[:, :, pl.ds(pl.multiple_of(h * HD, HD), HD)].reshape(rows_t, HD)
        scores = (
            lax.dot_general(key_block, q_h, (((1,), (1,)), ((), ())), preferred_element_type=F32)
            * scale
        )
        scores = jnp.where(visible, scores, NEG_FILL)
        top = jnp.max(scores, axis=0, keepdims=True)
        weights = jnp.where(visible, jnp.exp(scores - top), 0.0)
        total = jnp.sum(weights, axis=0, keepdims=True)
        numer = jnp.dot(value_t, weights.astype(BF16), preferred_element_type=F32)
        st_send[h, 0:1, :] = top
        st_send[h, 1:2, :] = total
        for c in range(per_head):
            num_send[h * per_head + c] = numer[c * cw : (c + 1) * cw].astype(BF16)
        for c in range(per_head):
            p = h * per_head + c

            @pl.when(p != b)
            def _():
                num_copy(p, b).start()
                st_copy(h, p, b).start()

    own_head = b // per_head

    def wait_table(j, carry):
        w_copy(b, peer(j)).wait_recv()
        return carry

    lax.fori_loop(1, n, wait_table, 0)
    table_forward = to_sibling(wbuf.at[r], wbuf.at[r], wf_sems.at[0], wf_sems.at[1])
    table_forward.start()

    num_recv[b] = num_send[b]
    st_recv[b] = st_send[own_head]

    def wait_partial(j, carry):
        num_copy(b, peer(j)).wait_recv()
        st_copy(own_head, b, peer(j)).wait_recv()
        return carry

    lax.fori_loop(1, n, wait_partial, 0)

    tops = st_recv[:, 0:1, :]
    sums = st_recv[:, 1:2, :]
    row_top = jnp.max(tops, axis=0, keepdims=True)
    factors = jnp.exp(tops - row_top)
    inverse = 1.0 / jnp.sum(factors * sums, axis=0)
    mixed = jnp.zeros((cw, rows_t), F32)
    for s in range(n):
        mixed = mixed + num_recv[s].astype(F32) * factors[s]
    attended = (mixed * inverse).T
    att_rows[...] = attended.reshape(n, 2, tokens, cw)

    loads[3].wait()
    half_rows = n * tokens
    att_other = att_rows[:, other].reshape(half_rows, cw).astype(BF16)
    att_mine = att_rows[:, r].reshape(half_rows, cw).astype(BF16)
    att_both = jnp.concatenate([att_other, att_mine], axis=0)

    def stacked(left, right):
        return jnp.concatenate(
            [left.reshape(n, tokens, part), right.reshape(n, tokens, part)], axis=1
        )

    def reduce_scatter(which, columns_of):
        copies = []
        for c in range(PARTS):
            left = columns_of(c * part)
            right = columns_of(half + c * part)
            sib_send[which, c] = stacked(left[:half_rows], right[:half_rows]).astype(BF16)
            copy = to_sibling(
                sib_send.at[which, c],
                sib_recv.at[which, c],
                sib_sems.at[which, 0, c],
                sib_sems.at[which, 1, c],
            )
            copy.start()
            copies.append(copy)
            acc[:, :, c * part : (c + 1) * part] = stacked(left[half_rows:], right[half_rows:])
        for copy in copies:
            copy.wait_recv()

        def summed(p):
            arrived = jnp.concatenate([sib_recv[which, c, p] for c in range(PARTS)], axis=1)
            return acc[p] + arrived.astype(F32)

        sems = red_sems.at[which]

        def red_copy(p, slot):
            return to_peer(red_send.at[which, p], red_recv.at[which, slot], sems, p, slot)

        def send(j, carry):
            p = peer(j)
            red_send[which, p] = summed(p).astype(BF16)
            red_copy(p, b).start()
            return carry

        lax.fori_loop(1, n, send, 0)

        def receive(j, running):
            p = peer(j)
            red_copy(b, p).wait_recv()
            return running + red_recv[which, p].astype(F32)

        result = lax.fori_loop(1, n, receive, summed(b))

        def finish():
            for copy in copies:
                copy.wait_send()

            def done(j, carry):
                red_copy(peer(j), b).wait_send()
                return carry

            lax.fori_loop(1, n, done, 0)

        return result, finish

    projected, finish_proj = reduce_scatter(
        0,
        lambda start: jnp.dot(
            att_both, owbuf[:, start : start + part], preferred_element_type=F32
        ),
    )

    def unstacked(values):
        return jnp.concatenate([values[:tokens], values[tokens:]], axis=1)

    attn_proj = unstacked(projected).astype(BF16)
    proj_ref[...] = attn_proj
    values_f = attn_proj.astype(F32)
    mean_square = jnp.mean(values_f * values_f, axis=-1, keepdims=True)
    gain = gain_ref[...].astype(F32).reshape(1, d_model)
    normed = values_f * lax.rsqrt(mean_square + EPSILON) * gain
    xbuf[r, b] = jnp.concatenate([normed[:, :half], normed[:, half:]], axis=0).astype(BF16)

    def x_copy(p, slot):
        return to_peer(xbuf.at[r, slot], xbuf.at[r, slot], x_sems, p, slot)

    def x_forward(side, slot):
        return to_sibling(
            xbuf.at[side, slot], xbuf.at[side, slot], fwd_sems.at[0, slot], fwd_sems.at[1, slot]
        )

    def send_x(j, carry):
        x_copy(peer(j), b).start()
        return carry

    lax.fori_loop(1, n, send_x, 0)
    x_forward(r, b).start()

    def pass_on(j, carry):
        p = peer(j)
        x_copy(b, p).wait_recv()
        x_forward(r, p).start()
        return carry

    lax.fori_loop(1, n, pass_on, 0)

    table_forward.wait_recv()
    expert = 2 * b + r
    lanes = lax.broadcasted_iota(jnp.int32, (half_rows, wbuf.shape[3]), 1)

    def weight_column(side):
        rows = wbuf[side].reshape(half_rows, wbuf.shape[3])
        return jnp.sum(jnp.where(lanes == expert, rows, 0.0), axis=1, keepdims=True)

    mix = jnp.concatenate([weight_column(other), weight_column(r)], axis=0)

    def lay_out(side, first):
        rows = xbuf[side].astype(F32).reshape(n, 2, tokens, half)
        xs[first : first + half_rows, :half] = rows[:, 0].reshape(half_rows, half).astype(BF16)
        xs[first : first + half_rows, half:] = rows[:, 1].reshape(half_rows, half).astype(BF16)

    lay_out(r, half_rows)
    loads[4].wait()
    loads[5].wait()

    def wait_forwarded(p, carry):
        x_forward(other, p).wait_recv()
        return carry

    lax.fori_loop(0, n, wait_forwarded, 0)
    lay_out(other, 0)

    everyone = xs[...]
    gate_part = jnp.dot(everyone, gbuf[...], preferred_element_type=F32)
    up_part = jnp.dot(everyone, ubuf[...], preferred_element_type=F32)
    hidden = (gate_part / (1.0 + jnp.exp(-gate_part)) * up_part).astype(BF16)
    loads[6].wait()

    def down_columns(start):
        result = jnp.dot(hidden, dbuf[:, start : start + part], preferred_element_type=F32)
        return result.astype(BF16).astype(F32) * mix

    blended, finish_down = reduce_scatter(1, down_columns)
    out_ref[...] = unstacked(blended).astype(BF16)

    def sent(j, carry):
        p = peer(j)
        q_copy(p, b).wait_send()
        w_copy(p, b).wait_send()
        num_copy(p, b).wait_send()
        st_copy(p // per_head, p, b).wait_send()
        x_copy(p, b).wait_send()
        return carry

    lax.fori_loop(1, n, sent, 0)

    def forwarded(p, carry):
        x_forward(r, p).wait_send()
        return carry

    lax.fori_loop(0, n, forwarded, 0)
    table_forward.wait_send()
    finish_proj()
    finish_down()


def solution(mesh):
    n = mesh.shape["blk"]

    def on_device(
        queries,
        cache_keys,
        cache_values,
        span_starts,
        out_weight,
        norm_gain,
        expert_ids,
        gate_fixed,
        gate_weight,
        up_weight,
        down_weight,
    ):
        own_q, width = queries.shape
        tokens, d_model = expert_ids.shape[0], out_weight.shape[1]
        rows_t = n * own_q
        heads = width // HD
        cw = width // n
        half = d_model // 2
        experts = 2 * n * gate_weight.shape[0]
        table_lanes = -(-experts // LANES) * LANES
        dma = pltpu.SemaphoreType.DMA
        anywhere = pl.BlockSpec(memory_space=pl.ANY)
        vmem = pl.BlockSpec(memory_space=pltpu.VMEM)
        smem = pl.BlockSpec(memory_space=pltpu.SMEM)
        out = jax.ShapeDtypeStruct((tokens, d_model), BF16)
        return pl.pallas_call(
            functools.partial(fused, n),
            out_shape=(out, out),
            in_specs=[
                anywhere,
                anywhere,
                anywhere,
                smem,
                anywhere,
                vmem,
                vmem,
                vmem,
                anywhere,
                anywhere,
                anywhere,
            ],
            out_specs=(vmem, vmem),
            scratch_shapes=[
                pltpu.VMEM((n, own_q, width), BF16),
                pltpu.VMEM(cache_keys.shape, BF16),
                pltpu.VMEM(cache_values.shape, BF16),
                pltpu.VMEM(out_weight.shape, BF16),
                pltpu.VMEM(gate_weight.shape[1:], BF16),
                pltpu.VMEM(up_weight.shape[1:], BF16),
                pltpu.VMEM(down_weight.shape[1:], BF16),
                pltpu.VMEM((2, n, tokens, table_lanes), F32),
                pltpu.VMEM((n, cw, rows_t), BF16),
                pltpu.VMEM((n, cw, rows_t), BF16),
                pltpu.VMEM((heads, 8, rows_t), F32),
                pltpu.VMEM((n, 8, rows_t), F32),
                pltpu.VMEM((n, 2, tokens, cw), F32),
                pltpu.VMEM((2, PARTS, n, 2 * tokens, half // PARTS), BF16),
                pltpu.VMEM((2, PARTS, n, 2 * tokens, half // PARTS), BF16),
                pltpu.VMEM((n, 2 * tokens, half), F32),
                pltpu.VMEM((2, n, 2 * tokens, half), BF16),
                pltpu.VMEM((2, n, 2 * tokens, half), BF16),
                pltpu.VMEM((2, n, 2 * tokens, half), BF16),
                pltpu.VMEM((rows_t, d_model), BF16),
                dma((7,)),
                dma((2, n)),
                dma((2, n)),
                dma((2, n)),
                dma((2, n)),
                dma((2, 2, n)),
                dma((2, n)),
                dma((2, n)),
                dma((2, 2, PARTS)),
                dma((2,)),
            ],
            compiler_params=pltpu.CompilerParams(
                collective_id=0, has_side_effects=True, vmem_limit_bytes=56 * 1024 * 1024
            ),
        )(
            queries,
            cache_keys,
            cache_values,
            span_starts,
            out_weight,
            norm_gain,
            expert_ids,
            gate_fixed,
            gate_weight,
            up_weight,
            down_weight,
        )

    in_specs = (
        P(("groups", "blk"), "rows"),
        P(("groups", "blk"), "rows"),
        P(("groups", "blk"), "rows"),
        P("groups"),
        P(("rows", "blk"), None),
        P(),
        P(("groups", "blk", "rows"), None),
        P(("groups", "blk", "rows"), None),
        P(("blk", "rows"), None, None),
        P(("blk", "rows"), None, None),
        P(("blk", "rows"), None, None),
    )
    out_specs = (P(("groups", "blk", "rows"), None), P(("groups", "blk", "rows"), None))
    return jax.shard_map(
        on_device, mesh=mesh, in_specs=in_specs, out_specs=out_specs, check_vma=False
    )
```

```python
import functools
import math

import jax
import jax.numpy as jnp
from jax import lax
from jax.experimental import pallas as pl
from jax.experimental.pallas import tpu as pltpu
from jax.sharding import PartitionSpec as P

HD = 128
NEG_FILL = -1e30
EPSILON = 1e-06
LANES = 128
PARTS = 2
MESH = pl.DeviceIdType.MESH
F32 = jnp.float32
BF16 = jnp.bfloat16


def fused(
    n,
    q_hbm,
    k_hbm,
    v_hbm,
    starts,
    ow_hbm,
    gain_ref,
    ids_ref,
    gates_ref,
    g_hbm,
    u_hbm,
    d_hbm,
    both_ref,
    qbuf,
    kbuf,
    vbuf,
    owbuf,
    gbuf,
    ubuf,
    dbuf,
    wbuf,
    num_send,
    num_recv,
    st_send,
    st_recv,
    att_rows,
    sib_send,
    sib_recv,
    acc,
    red_send,
    red_recv,
    xbuf,
    xs,
    local_sem,
    q_sems,
    w_sems,
    num_sems,
    st_sems,
    red_sems,
    x_sems,
    fwd_sems,
    sib_sems,
    wf_sems,
):
    b = lax.axis_index("blk")
    r = lax.axis_index("rows")
    other = 1 - r
    own_q, width = q_hbm.shape
    rows_t = n * own_q
    tokens = own_q // 2
    heads = width // HD
    cw = width // n
    per_head = HD // cw
    keys = k_hbm.shape[0]
    d_model = ow_hbm.shape[1]
    half = d_model // 2
    part = half // PARTS
    spans = starts.shape[0]

    def peer(j):
        return lax.rem(b + j, n)

    loads = [
        pltpu.make_async_copy(src, dst, local_sem.at[i])
        for i, (src, dst) in enumerate(
            (
                (q_hbm, qbuf.at[b]),
                (k_hbm, kbuf),
                (v_hbm, vbuf),
                (ow_hbm, owbuf),
                (g_hbm.at[0], gbuf),
                (u_hbm.at[0], ubuf),
                (d_hbm.at[0], dbuf),
            )
        )
    ]
    for load in loads:
        load.start()

    barrier = pltpu.get_barrier_semaphore()

    def greet(j, carry):
        pl.semaphore_signal(barrier, inc=1, device_id={"blk": peer(j)}, device_id_type=MESH)
        return carry

    lax.fori_loop(1, n, greet, 0)
    pl.semaphore_signal(barrier, inc=1, device_id={"rows": other}, device_id_type=MESH)

    gates = gates_ref[...].astype(F32)
    share = gates / jnp.sum(gates, axis=1, keepdims=True)
    ids = ids_ref[...]
    lane = lax.broadcasted_iota(jnp.int32, wbuf.shape[2:], 1)
    table = jnp.zeros(wbuf.shape[2:], F32)
    for k in range(ids_ref.shape[1]):
        table = table + jnp.where(ids[:, k : k + 1] == lane, share[:, k : k + 1], 0.0)
    wbuf[r, b] = table

    pl.semaphore_wait(barrier, n)

    def to_peer(src, dst, sems, p, slot):
        return pltpu.make_async_remote_copy(
            src_ref=src,
            dst_ref=dst,
            send_sem=sems.at[0, p],
            recv_sem=sems.at[1, slot],
            device_id={"blk": p},
            device_id_type=MESH,
        )

    def to_sibling(src, dst, send_sem, recv_sem):
        return pltpu.make_async_remote_copy(
            src_ref=src,
            dst_ref=dst,
            send_sem=send_sem,
            recv_sem=recv_sem,
            device_id={"rows": other},
            device_id_type=MESH,
        )

    def q_copy(p, slot):
        return to_peer(q_hbm, qbuf.at[slot], q_sems, p, slot)

    def w_copy(p, slot):
        return to_peer(wbuf.at[r, slot], wbuf.at[r, slot], w_sems, p, slot)

    def send_queries(j, carry):
        q_copy(peer(j), b).start()
        return carry

    def send_table(j, carry):
        w_copy(peer(j), b).start()
        return carry

    lax.fori_loop(1, n, send_queries, 0)
    lax.fori_loop(1, n, send_table, 0)

    loads[0].wait()
    loads[1].wait()
    loads[2].wait()
    key_block = kbuf[...]
    value_t = vbuf[...].T

    token = lax.broadcasted_iota(jnp.int32, (1, rows_t), 1)
    span_len = rows_t // spans
    start_of = jnp.zeros((1, rows_t), jnp.int32)
    for s in range(spans):
        start_of = jnp.where(token // span_len == s, starts[s], start_of)
    query_pos = start_of + lax.rem(token, span_len)
    limit = query_pos - b * keys
    visible = lax.broadcasted_iota(jnp.int32, (keys, rows_t), 0) <= limit

    def wait_queries(j, carry):
        q_copy(b, peer(j)).wait_recv()
        return carry

    lax.fori_loop(1, n, wait_queries, 0)

    def num_copy(p, slot):
        return to_peer(num_send.at[p], num_recv.at[slot], num_sems, p, slot)

    def st_copy(h, p, slot):
        return to_peer(st_send.at[h], st_recv.at[slot], st_sems, p, slot)

    scale = 1.0 / math.sqrt(HD)
    for j in range(heads):
        h = lax.rem(b // per_head + 1 + j, heads)
        q_h = qbuf[:, :, pl.ds(pl.multiple_of(h * HD, HD), HD)].reshape(rows_t, HD)
        scores = (
            lax.dot_general(key_block, q_h, (((1,), (1,)), ((), ())), preferred_element_type=F32)
            * scale
        )
        scores = jnp.where(visible, scores, NEG_FILL)
        top = jnp.max(scores, axis=0, keepdims=True)
        weights = jnp.where(visible, jnp.exp(scores - top), 0.0)
        total = jnp.sum(weights, axis=0, keepdims=True)
        numer = jnp.dot(value_t, weights.astype(BF16), preferred_element_type=F32)
        st_send[h, 0:1, :] = top
        st_send[h, 1:2, :] = total
        for c in range(per_head):
            num_send[h * per_head + c] = numer[c * cw : (c + 1) * cw].astype(BF16)
        for c in range(per_head):
            p = h * per_head + c

            @pl.when(p != b)
            def _():
                num_copy(p, b).start()
                st_copy(h, p, b).start()

    own_head = b // per_head

    def wait_table(j, carry):
        w_copy(b, peer(j)).wait_recv()
        return carry

    lax.fori_loop(1, n, wait_table, 0)
    table_forward = to_sibling(wbuf.at[r], wbuf.at[r], wf_sems.at[0], wf_sems.at[1])
    table_forward.start()

    num_recv[b] = num_send[b]
    st_recv[b] = st_send[own_head]

    def wait_partial(j, carry):
        num_copy(b, peer(j)).wait_recv()
        st_copy(own_head, b, peer(j)).wait_recv()
        return carry

    lax.fori_loop(1, n, wait_partial, 0)

    tops = st_recv[:, 0:1, :]
    sums = st_recv[:, 1:2, :]
    row_top = jnp.max(tops, axis=0, keepdims=True)
    factors = jnp.exp(tops - row_top)
    inverse = 1.0 / jnp.sum(factors * sums, axis=0)
    mixed = jnp.zeros((cw, rows_t), F32)
    for s in range(n):
        mixed = mixed + num_recv[s].astype(F32) * factors[s]
    attended = (mixed * inverse).T
    att_rows[...] = attended.reshape(n, 2, tokens, cw)

    loads[3].wait()
    half_rows = n * tokens
    att_other = att_rows[:, other].reshape(half_rows, cw).astype(BF16)
    att_mine = att_rows[:, r].reshape(half_rows, cw).astype(BF16)
    att_both = jnp.concatenate([att_other, att_mine], axis=0)

    def stacked(left, right):
        return jnp.concatenate(
            [left.reshape(n, tokens, part), right.reshape(n, tokens, part)], axis=1
        )

    def reduce_scatter(which, columns_of):
        copies = []
        for c in range(PARTS):
            left = columns_of(c * part)
            right = columns_of(half + c * part)
            sib_send[which, c] = stacked(left[:half_rows], right[:half_rows]).astype(BF16)
            copy = to_sibling(
                sib_send.at[which, c],
                sib_recv.at[which, c],
                sib_sems.at[which, 0, c],
                sib_sems.at[which, 1, c],
            )
            copy.start()
            copies.append(copy)
            acc[:, :, c * part : (c + 1) * part] = stacked(left[half_rows:], right[half_rows:])
        for copy in copies:
            copy.wait_recv()

        def summed(p):
            arrived = jnp.concatenate([sib_recv[which, c, p] for c in range(PARTS)], axis=1)
            return acc[p] + arrived.astype(F32)

        sems = red_sems.at[which]

        def red_copy(p, slot):
            return to_peer(red_send.at[which, p], red_recv.at[which, slot], sems, p, slot)

        def send(j, carry):
            p = peer(j)
            red_send[which, p] = summed(p).astype(BF16)
            red_copy(p, b).start()
            return carry

        lax.fori_loop(1, n, send, 0)

        def receive(j, running):
            p = peer(j)
            red_copy(b, p).wait_recv()
            return running + red_recv[which, p].astype(F32)

        result = lax.fori_loop(1, n, receive, summed(b))

        def finish():
            for copy in copies:
                copy.wait_send()

            def done(j, carry):
                red_copy(peer(j), b).wait_send()
                return carry

            lax.fori_loop(1, n, done, 0)

        return result, finish

    projected, finish_proj = reduce_scatter(
        0,
        lambda start: jnp.dot(
            att_both, owbuf[:, start : start + part], preferred_element_type=F32
        ),
    )

    def unstacked(values):
        return jnp.concatenate([values[:tokens], values[tokens:]], axis=1)

    attn_proj = unstacked(projected).astype(BF16)
    values_f = attn_proj.astype(F32)
    both_ref[:tokens] = values_f
    mean_square = jnp.mean(values_f * values_f, axis=-1, keepdims=True)
    gain = gain_ref[...].astype(F32).reshape(1, d_model)
    normed = values_f * lax.rsqrt(mean_square + EPSILON) * gain
    xbuf[r, b] = jnp.concatenate([normed[:, :half], normed[:, half:]], axis=0).astype(BF16)

    def x_copy(p, slot):
        return to_peer(xbuf.at[r, slot], xbuf.at[r, slot], x_sems, p, slot)

    def x_forward(side, slot):
        return to_sibling(
            xbuf.at[side, slot], xbuf.at[side, slot], fwd_sems.at[0, slot], fwd_sems.at[1, slot]
        )

    def send_x(j, carry):
        x_copy(peer(j), b).start()
        return carry

    lax.fori_loop(1, n, send_x, 0)
    x_forward(r, b).start()

    def pass_on(j, carry):
        p = peer(j)
        x_copy(b, p).wait_recv()
        x_forward(r, p).start()
        return carry

    lax.fori_loop(1, n, pass_on, 0)

    table_forward.wait_recv()
    expert = 2 * b + r
    lanes = lax.broadcasted_iota(jnp.int32, (half_rows, wbuf.shape[3]), 1)

    def weight_column(side):
        rows = wbuf[side].reshape(half_rows, wbuf.shape[3])
        return jnp.sum(jnp.where(lanes == expert, rows, 0.0), axis=1, keepdims=True)

    mix = jnp.concatenate([weight_column(other), weight_column(r)], axis=0)

    def lay_out(side, first):
        rows = xbuf[side].astype(F32).reshape(n, 2, tokens, half)
        xs[first : first + half_rows, :half] = rows[:, 0].reshape(half_rows, half).astype(BF16)
        xs[first : first + half_rows, half:] = rows[:, 1].reshape(half_rows, half).astype(BF16)

    lay_out(r, half_rows)
    loads[4].wait()
    loads[5].wait()

    def wait_forwarded(p, carry):
        x_forward(other, p).wait_recv()
        return carry

    lax.fori_loop(0, n, wait_forwarded, 0)
    lay_out(other, 0)

    everyone = xs[...]
    gate_part = jnp.dot(everyone, gbuf[...], preferred_element_type=F32)
    up_part = jnp.dot(everyone, ubuf[...], preferred_element_type=F32)
    hidden = (gate_part / (1.0 + jnp.exp(-gate_part)) * up_part).astype(BF16)
    loads[6].wait()

    def down_columns(start):
        result = jnp.dot(hidden, dbuf[:, start : start + part], preferred_element_type=F32)
        return result.astype(BF16).astype(F32) * mix

    blended, finish_down = reduce_scatter(1, down_columns)
    both_ref[tokens:] = unstacked(blended)

    def sent(j, carry):
        p = peer(j)
        q_copy(p, b).wait_send()
        w_copy(p, b).wait_send()
        num_copy(p, b).wait_send()
        st_copy(p // per_head, p, b).wait_send()
        x_copy(p, b).wait_send()
        return carry

    lax.fori_loop(1, n, sent, 0)

    def forwarded(p, carry):
        x_forward(r, p).wait_send()
        return carry

    lax.fori_loop(0, n, forwarded, 0)
    table_forward.wait_send()
    finish_proj()
    finish_down()


def solution(mesh):
    n = mesh.shape["blk"]

    def on_device(
        queries,
        cache_keys,
        cache_values,
        span_starts,
        out_weight,
        norm_gain,
        expert_ids,
        gate_fixed,
        gate_weight,
        up_weight,
        down_weight,
    ):
        own_q, width = queries.shape
        tokens, d_model = expert_ids.shape[0], out_weight.shape[1]
        rows_t = n * own_q
        heads = width // HD
        cw = width // n
        half = d_model // 2
        experts = 2 * n * gate_weight.shape[0]
        table_lanes = -(-experts // LANES) * LANES
        dma = pltpu.SemaphoreType.DMA
        anywhere = pl.BlockSpec(memory_space=pl.ANY)
        vmem = pl.BlockSpec(memory_space=pltpu.VMEM)
        smem = pl.BlockSpec(memory_space=pltpu.SMEM)
        both = pl.pallas_call(
            functools.partial(fused, n),
            out_shape=jax.ShapeDtypeStruct((2 * tokens, d_model), F32),
            in_specs=[
                anywhere,
                anywhere,
                anywhere,
                smem,
                anywhere,
                vmem,
                vmem,
                vmem,
                anywhere,
                anywhere,
                anywhere,
            ],
            out_specs=vmem,
            scratch_shapes=[
                pltpu.VMEM((n, own_q, width), BF16),
                pltpu.VMEM(cache_keys.shape, BF16),
                pltpu.VMEM(cache_values.shape, BF16),
                pltpu.VMEM(out_weight.shape, BF16),
                pltpu.VMEM(gate_weight.shape[1:], BF16),
                pltpu.VMEM(up_weight.shape[1:], BF16),
                pltpu.VMEM(down_weight.shape[1:], BF16),
                pltpu.VMEM((2, n, tokens, table_lanes), F32),
                pltpu.VMEM((n, cw, rows_t), BF16),
                pltpu.VMEM((n, cw, rows_t), BF16),
                pltpu.VMEM((heads, 8, rows_t), F32),
                pltpu.VMEM((n, 8, rows_t), F32),
                pltpu.VMEM((n, 2, tokens, cw), F32),
                pltpu.VMEM((2, PARTS, n, 2 * tokens, half // PARTS), BF16),
                pltpu.VMEM((2, PARTS, n, 2 * tokens, half // PARTS), BF16),
                pltpu.VMEM((n, 2 * tokens, half), F32),
                pltpu.VMEM((2, n, 2 * tokens, half), BF16),
                pltpu.VMEM((2, n, 2 * tokens, half), BF16),
                pltpu.VMEM((2, n, 2 * tokens, half), BF16),
                pltpu.VMEM((rows_t, d_model), BF16),
                dma((7,)),
                dma((2, n)),
                dma((2, n)),
                dma((2, n)),
                dma((2, n)),
                dma((2, 2, n)),
                dma((2, n)),
                dma((2, n)),
                dma((2, 2, PARTS)),
                dma((2,)),
            ],
            compiler_params=pltpu.CompilerParams(
                collective_id=0, has_side_effects=True, vmem_limit_bytes=56 * 1024 * 1024
            ),
        )(
            queries,
            cache_keys,
            cache_values,
            span_starts,
            out_weight,
            norm_gain,
            expert_ids,
            gate_fixed,
            gate_weight,
            up_weight,
            down_weight,
        )
        return both[:tokens].astype(BF16), both[tokens:].astype(BF16)

    in_specs = (
        P(("groups", "blk"), "rows"),
        P(("groups", "blk"), "rows"),
        P(("groups", "blk"), "rows"),
        P("groups"),
        P(("rows", "blk"), None),
        P(),
        P(("groups", "blk", "rows"), None),
        P(("groups", "blk", "rows"), None),
        P(("blk", "rows"), None, None),
        P(("blk", "rows"), None, None),
        P(("blk", "rows"), None, None),
    )
    out_specs = (P(("groups", "blk", "rows"), None), P(("groups", "blk", "rows"), None))
    return jax.shard_map(
        on_device, mesh=mesh, in_specs=in_specs, out_specs=out_specs, check_vma=False
    )
```
